512 devices in a mesh: ctx: 64 (over x, z), head: 8 (over y, core).
Axes of the slice: x: 4, y: 4, z: 16, core: 2. Of those that a mesh axis runs over, the one named last changes fastest.
Arguments:
- lin_queries: bfloat16 [8192, 4096], P('ctx', 'head'), may hold values from -6 to 6
- lin_keys: bfloat16 [8192, 4096], P('ctx', 'head'), may hold values from -6 to 6
- lin_values: bfloat16 [8192, 4096], P('ctx', 'head'), may hold values from -6 to 6
- state_in: float32 [32, 128, 128], P('head'), may hold values from -24 to 24
- decay_exps: int32 [32], P('head'), may hold values from 5 to 13
- soft_queries: bfloat16 [8192, 4096], P('ctx', 'head'), may hold values from -80 to 80
- soft_keys: bfloat16 [8192, 1024], P('ctx', 'head'), may hold values from -4 to 4
- soft_values: bfloat16 [8192, 1024], P('ctx', 'head'), may hold values from -6 to 6
- lin_gain: float32 [4096], P('head'), may hold values from 0.5 to 1.5
- soft_gain: float32 [4096], P('head'), may hold values from 0.5 to 1.5
- lin_weight: bfloat16 [4096, 3072], P(('head', 'ctx')), may hold values from -0.09375 to 0.09375
- soft_weight: bfloat16 [4096, 3072], P(('head', 'ctx')), may hold values from -0.09375 to 0.09375
Outputs:
- lin_projected: bfloat16 [8192, 3072], P('ctx', 'head')
- soft_projected: bfloat16 [8192, 3072], P('ctx', 'head')
The draws below stay inside these ranges and needn't reach their ends.
All inputs are finite; a program needn't handle non-finite values.
Results may differ from the reference program's by a relative error of at most 0.019.
Values may be sent and summed in bfloat16 or wider, within the bound.
A program may use at most 128 MiB of HBM per device.

```python
import jax
import jax.numpy as jnp
from jax import lax

HEADS = 32
KV_HEADS = 8
HEAD_DIM = 128
DOUT = 3072
TOK_DEV = 128
TOKENS = 8192
N_CTX = 64


def shared_keys(key):
    base = jax.random.normal(jax.random.fold_in(key, 11), (TOKENS, KV_HEADS, HEAD_DIM), jnp.float32)
    return jnp.clip(base, -4.0, 4.0)


def draw_soft_keys(key, part):
    key = jax.random.fold_in(key, 3)
    base = shared_keys(key)
    return base.reshape(TOKENS, KV_HEADS * HEAD_DIM).astype(jnp.bfloat16)


def draw_soft_queries(key, part):
    own_key = jax.random.fold_in(key, 5)
    queries = jnp.clip(jax.random.normal(own_key, (TOKENS, HEADS, HEAD_DIM), jnp.float32), -6.0, 6.0)
    return queries.reshape(TOKENS, HEADS * HEAD_DIM).astype(jnp.bfloat16)


def plant(values, key, least, largest):
    extent = values.shape
    place = [jax.random.randint(jax.random.fold_in(key, axis), (), 0, extent[axis]) for axis in range(len(extent))]
    values = values.at[tuple(place)].set(least)
    longest = extent.index(max(extent))
    place[longest] = (place[longest] + 1) % extent[longest]
    return values.at[tuple(place)].set(largest)


def level_of(stream_key, dims, split, smallest, largest):
    factor_of, own = 1.0, jax.random.fold_in(stream_key, 6)
    for axis_at, blocks in split:
        heights = jnp.exp(jax.random.uniform(jax.random.fold_in(own, axis_at), (blocks,), jnp.float32, smallest / len(split), largest / len(split)))
        factor_of = factor_of * jnp.repeat(heights, dims[axis_at] // blocks).reshape([-1 if axis == axis_at else 1 for axis in range(len(dims))])
    return factor_of


def normal_values(key, dims, deviation, most, cuts=(), held_as=jnp.bfloat16):
    factor_of = level_of(key, dims, cuts, -0.22, 0.18) if cuts else 1.0
    result = jax.random.normal(key, dims, jnp.float32) * deviation * factor_of
    return jnp.minimum(jnp.maximum(result, -most), most).astype(held_as)


def setup_inputs(seed: int = 0) -> dict:
    splits = jax.random.split(jax.random.key(seed), 13)
    return {
        "lin_queries": normal_values(splits[0], (TOKENS, HEADS * HEAD_DIM), 1.0, 6.0, ((0, 64), (1, 8))),
        "lin_keys": normal_values(splits[1], (TOKENS, HEADS * HEAD_DIM), 1.0, 6.0, ((0, 64), (1, 8))),
        "lin_values": normal_values(splits[2], (TOKENS, HEADS * HEAD_DIM), 1.0, 6.0, ((0, 64), (1, 8))),
        "state_in": normal_values(splits[3], (HEADS, HEAD_DIM, HEAD_DIM), 4.0, 24.0, ((0, 8),), jnp.float32),
        "decay_exps": plant(jax.random.randint(splits[4], (HEADS,), 5, 14), jax.random.fold_in(splits[4], 1), 5, 13).astype(jnp.int32),
        "soft_queries": draw_soft_queries(jax.random.fold_in(splits[12], 71), 0),
        "soft_keys": draw_soft_keys(jax.random.fold_in(splits[12], 71), 0),
        "soft_values": normal_values(splits[7], (TOKENS, KV_HEADS * HEAD_DIM), 1.0, 6.0, ((0, 64), (1, 8))),
        "lin_gain": jnp.clip(1.0 + 0.1 * jax.random.normal(splits[8], (HEADS * HEAD_DIM,), jnp.float32), 0.5, 1.5),
        "soft_gain": jnp.clip(1.0 + 0.1 * jax.random.normal(splits[9], (HEADS * HEAD_DIM,), jnp.float32), 0.5, 1.5),
        "lin_weight": normal_values(splits[10], (HEADS * HEAD_DIM, DOUT), (HEADS * HEAD_DIM) ** -0.5, 0.09375, ((0, 512),)),
        "soft_weight": normal_values(splits[11], (HEADS * HEAD_DIM, DOUT), (HEADS * HEAD_DIM) ** -0.5, 0.09375, ((0, 512),)),
    }


HIGH = lax.Precision.HIGHEST

def branch_norm(values, gain):
    scale = lax.rsqrt(lax.optimization_barrier(jnp.mean(values * values, axis=-1, keepdims=True)) + 1e-06)
    return values * scale * gain.reshape(values.shape[-2], values.shape[-1])

def lightning_tables(rates, block):
    offsets = jnp.arange(block).astype(jnp.float32)
    within = offsets[:, None] - offsets[None, :]
    causal = within >= 0
    inside = jnp.where(causal[None], jnp.exp(-rates[:, None, None] * jnp.maximum(within, 0.0)[None]), 0.0)
    query_decay = jnp.exp(-rates[None, :] * (offsets[:, None] + 1.0))
    key_decay = jnp.exp(-rates[None, :] * (block - 1.0 - offsets[:, None]))
    block_decay = jnp.exp(-rates * block)
    return (inside, query_decay, key_decay, block_decay)

def lightning_block(queries, keys, values, state, tables):
    inside, query_decay, key_decay, block_decay = tables
    scores = jnp.einsum('thd,uhd->htu', queries, keys, precision=HIGH) * inside
    intra = jnp.einsum('htu,uhd->thd', scores, values, precision=HIGH)
    inter = jnp.einsum('thd,hde->the', queries * query_decay[:, :, None], state, precision=HIGH)
    update = jnp.einsum('uhd,uhe->hde', keys * key_decay[:, :, None], values, precision=HIGH)
    return (intra + inter, update, block_decay)

def reference(lin_queries, lin_keys, lin_values, state_in, decay_exps, soft_queries, soft_keys, soft_values, lin_gain, soft_gain, lin_weight, soft_weight):
    rates = jnp.exp2(-decay_exps.astype(jnp.float32))
    tables = lightning_tables(rates, TOK_DEV)

    def shaped(array):
        return array.astype(jnp.float32).reshape(N_CTX, TOK_DEV, HEADS, HEAD_DIM)

    def advance(state, block):
        queries, keys, values = block
        output, update, block_decay = lightning_block(queries, keys, values, state, tables)
        return (block_decay[:, None, None] * state + update, output)
    final_state, lin_out = lax.scan(advance, state_in, (shaped(lin_queries), shaped(lin_keys), shaped(lin_values)))
    lin_norm = branch_norm(lin_out.reshape(TOKENS, HEADS, HEAD_DIM), lin_gain)
    lin_norm = lin_norm.reshape(TOKENS, HEADS * HEAD_DIM).astype(jnp.bfloat16)
    lin_projected = jnp.dot(lin_norm, lin_weight, preferred_element_type=jnp.float32).astype(jnp.bfloat16)
    group = HEADS // KV_HEADS
    qblock = min(512, TOKENS)
    nblocks = TOKENS // qblock
    all_queries = soft_queries.astype(jnp.float32).reshape(nblocks, qblock, KV_HEADS, group, HEAD_DIM)
    all_keys = soft_keys.astype(jnp.float32).reshape(TOKENS, KV_HEADS, HEAD_DIM)
    all_values = soft_values.astype(jnp.float32).reshape(TOKENS, KV_HEADS, HEAD_DIM)
    key_positions = jnp.arange(TOKENS)
    factor = 1.0 / HEAD_DIM ** 0.5

    def attend(index):
        block_index = index // KV_HEADS
        kv_index = index % KV_HEADS
        queries = all_queries[block_index, :, kv_index]
        keys = all_keys[:, kv_index]
        values = all_values[:, kv_index]
        scores = jnp.einsum('qgd,kd->gqk', queries, keys) * factor
        query_positions = block_index * qblock + jnp.arange(qblock)
        causal = key_positions[None, :] <= query_positions[:, None]
        scores = jnp.where(causal[None], scores, -1e+30)
        peak = lax.optimization_barrier(jnp.max(scores, axis=-1, keepdims=True))
        weights = jnp.where(causal[None], jnp.exp(scores - peak), 0.0)
        totals = lax.optimization_barrier(jnp.sum(weights, axis=-1))
        rounded = weights.astype(jnp.bfloat16).astype(jnp.float32)
        summed = jnp.einsum('gqk,kd->qgd', rounded, values)
        return summed / jnp.transpose(totals)[:, :, None]
    pieces = lax.map(attend, jnp.arange(nblocks * KV_HEADS))
    soft_out = pieces.reshape(nblocks, KV_HEADS, qblock, group, HEAD_DIM)
    soft_out = jnp.transpose(soft_out, (0, 2, 1, 3, 4)).reshape(TOKENS, HEADS, HEAD_DIM)
    soft_norm = branch_norm(soft_out, soft_gain).reshape(TOKENS, HEADS * HEAD_DIM).astype(jnp.bfloat16)
    soft_projected = jnp.dot(soft_norm, soft_weight, preferred_element_type=jnp.float32).astype(jnp.bfloat16)
    return (lin_projected, soft_projected)
```

```python
import functools

import jax
import jax.numpy as jnp
from jax import lax
from jax.experimental import pallas as pl
from jax.experimental.pallas import tpu as pltpu
from jax.sharding import PartitionSpec as P

D = 128
H = 4
TOK = 128
NOUT = 384
MESH = pl.DeviceIdType.MESH
BF = jnp.bfloat16
F32 = jnp.float32
NEG = -1e30
FLOOR = -1e29


def dot(a, b):
    return jnp.dot(a, b, preferred_element_type=F32)


def dot_t(a, b):
    return lax.dot_general(a, b, (((1,), (1,)), ((), ())), preferred_element_type=F32)


def split2(a):
    hi = a.astype(BF)
    return hi, (a - hi.astype(F32)).astype(BF)


def iota(shape, axis):
    return lax.broadcasted_iota(jnp.int32, shape, axis)


def head_norm(values, gain):
    scale = lax.rsqrt(jnp.mean(values * values, axis=-1, keepdims=True) + 1e-06)
    return values * scale * gain


def kernel(
    nx, nz, lq, lk, lv, st, de, sq, sk, sv, lg, sg, lw, sw, lo, so,
    kvst, kvg, qst, qh, wst, wland, wg, us, uland, tx, ss, sland,
    osend, oland, lsend, lland, ag, csend, cland, perm, bias,
    kvt_s, kvt_r, wt_s, wt_r, qt_s, qt_r, ua_s, ua_r, tx_s, tx_r, sa_s, sa_r,
    kv_s, kv_r, wr_s, wr_r, os_s, os_r, ls_s, ls_r, lat_s, lat_r, sat_s, sat_r,
    fw_s, fw_r, cs_s, cs_r,
):
    ny = nx
    half = nz // 2
    rows = lw.shape[0]
    sub = TOK // ny
    span = nz * sub
    depth = H * D
    part = depth // nz
    ctx, head = lax.axis_index("ctx"), lax.axis_index("head")
    x, z = ctx // nz, ctx % nz
    y, c = head // 2, head % 2

    def dev(dx, dy, dz, dc):
        return (dx * nz + dz, dy * 2 + dc)

    def remote(src, dst, ssem, rsem, to):
        return pltpu.make_async_remote_copy(
            src_ref=src, dst_ref=dst, send_sem=ssem, recv_sem=rsem, device_id=to, device_id_type=MESH
        )

    on_diag = x == y

    barrier = pltpu.get_barrier_semaphore()

    def greet(to):
        pl.semaphore_signal(barrier, inc=1, device_id=to, device_id_type=MESH)

    def greet_z(i, carry):
        greet(dev(x, y, (z + i) % nz, c))
        return carry

    lax.fori_loop(1, nz, greet_z, 0)
    for i in range(1, nx):
        greet(dev((x + i) % nx, y, z, c))
        greet(dev(x, (y + i) % ny, z, c))
    greet(dev(x, y, z, 1 - c))
    for i in range(nx):
        if i == 0:

            @pl.when(jnp.logical_not(on_diag))
            def _():
                greet(dev(x, x, z, c))

        else:
            greet(dev((x + i) % nx, x, z, c))
        greet(dev((x + i) % nx, x, z, 1 - c))

    for j in range(ny):
        kvst[j, 0] = sk[j * sub : (j + 1) * sub, :]
        kvst[j, 1] = sv[j * sub : (j + 1) * sub, :]
    for h in range(H):
        qst[h * TOK : (h + 1) * TOK, :] = sq[:, h * D : (h + 1) * D]
    gain = jnp.concatenate([sg[:, h * D : (h + 1) * D] for h in range(H)], axis=0)
    g0 = gain.astype(BF).astype(F32)
    g1 = (gain - g0).astype(BF).astype(F32)
    g2 = gain - g0 - g1
    qst[H * TOK :, :] = jnp.concatenate([g0, g1, g2, jnp.zeros_like(g0)], axis=0).astype(BF)
    for layer, ref in ((0, lw), (1, sw)):
        wide = ref[...].astype(F32)
        for j in range(ny):
            for k in range(2):
                at = (j * 2 + k) * NOUT
                wst[j, k, layer] = wide[:, at : at + NOUT]

    def rate_of(e):
        return jnp.exp2(-jnp.full((8, D), e, jnp.int32).astype(F32))[:1]

    for h in range(H):
        rate = rate_of(de[h])
        back = (TOK - 1 - iota((TOK, D), 0)).astype(F32)
        scaled = lk[:, h * D : (h + 1) * D].astype(F32) * jnp.exp(-rate * back)
        hi, lo_ = split2(scaled.T)
        v = lv[:, h * D : (h + 1) * D]
        update = (dot(hi, v) + dot(lo_, v)).astype(BF)
        per = D // part
        for k in range(per):
            us[h * per + k] = update[k * part : (k + 1) * part, :]

    n_greet = (nz - 1) + 2 * (nx - 1) + 1 + 2 * nx - jnp.where(on_diag, 1, 0)
    pl.semaphore_wait(barrier, n_greet)

    def plane_send(src, dst, ssem, rsem, i, other=False):
        j = (y + i) % ny
        to = dev(y, j, z, 1 - c if other else c)
        if i == 0 and not other:

            @pl.when(on_diag)
            def _():
                pltpu.make_async_copy(src, dst, rsem).start()

            @pl.when(jnp.logical_not(on_diag))
            def _():
                remote(src, dst, ssem, rsem, to).start()

        else:
            remote(src, dst, ssem, rsem, to).start()

    def plane_sent(src, ssem, i, other=False):
        if i == 0 and not other:

            @pl.when(jnp.logical_not(on_diag))
            def _():
                pltpu.make_async_copy(src, src, ssem).wait()

        else:
            pltpu.make_async_copy(src, src, ssem).wait()

    def landed(dst, rsem):
        pltpu.make_async_copy(dst, dst, rsem).wait()

    for i in range(ny):
        plane_send(kvst.at[(y + i) % ny], kvg.at[:, x, 0], kvt_s.at[i], kvt_r.at[x], i)

    def u_copy(i):
        to = (z + i) % nz
        return remote(us.at[to], uland.at[z], ua_s.at[i], ua_r.at[i], dev(x, y, to, c))

    def u_start(i, carry):
        u_copy(i).start()
        return carry

    lax.fori_loop(1, nz, u_start, 0)
    for i in range(ny):
        for k in range(2):
            other = k == 1
            plane_send(
                wst.at[(y + i) % ny, 1 - c if other else c],
                wland.at[c, x], wt_s.at[k, i], wt_r.at[k, x], i, other,
            )
    for i in range(ny):
        plane_send(qst, qh.at[x], qt_s.at[i], qt_r.at[x], i)
    uland[z] = us[z]

    def kv_steps(stream, way):
        return half if stream == way else half - 1

    def kv_copy(stream, way, s):
        if way == 0:
            src, dst, to = (0 if s == 1 else 2 * s - 3), 2 * s - 1, (z + 1) % nz
        else:
            src, dst, to = 2 * s - 2, min(2 * s, nz - 1), (z + nz - 1) % nz
        return remote(
            kvg.at[stream, :, src], kvg.at[stream, :, dst],
            kv_s.at[stream, way, s - 1], kv_r.at[stream, way, s - 1], dev(x, y, to, c),
        )

    def w_copy(stream, way, s):
        if way == 0:
            at, to = (z + nz - s + 1) % nz, (z + 1) % nz
        else:
            at, to = (z + s - 1) % nz, (z + nz - 1) % nz
        block = wg.at[stream, :, at]
        return remote(
            block, block, wr_s.at[stream, way, s - 1], wr_r.at[stream, way, s - 1], dev(x, y, to, c)
        )

    def ring(copy, s):
        for stream in range(2):
            for way in range(2):
                if s > 0 and s <= kv_steps(stream, way):
                    copy(stream, way, s).wait_recv()
                if s + 1 <= kv_steps(stream, way):
                    copy(stream, way, s + 1).start()

    for i in range(nx):
        landed(kvg.at[:, i, 0], kvt_r.at[i])
    ring(kv_copy, 0)
    for k in range(2):
        for i in range(nx):
            landed(wland.at[0, i], wt_r.at[k, i])
    for layer in range(2):
        for k in range(2):
            slab = jnp.concatenate([wland[k, i, layer] for i in range(nx)], axis=0)
            wg[layer, k, z] = slab.astype(BF)
    ring(w_copy, 0)

    def u_wait(i, carry):
        u_copy(i).wait_recv()
        return carry

    lax.fori_loop(1, nz, u_wait, 0)
    own = z * part // D
    lam = rate_of(de[own]) * float(TOK)
    step = jnp.exp(-lam)
    total = jnp.zeros((part, D), F32)
    before = []
    for i in range(nz):
        before.append(total)
        total = step * total + uland[i].astype(F32)
    tx[x] = total

    def tx_copy(i):
        return remote(tx.at[x], tx.at[x], tx_s.at[i], tx_r.at[i], dev((x + i) % nx, y, z, c))

    for i in range(1, nx):
        tx_copy(i).start()

    ring(kv_copy, 1)
    ring(w_copy, 1)

    for i in range(1, nx):
        tx_copy(i).wait_recv()
    xf = jnp.full((8, D), x, jnp.int32).astype(F32)[:1]
    first = pl.multiple_of((z * part) % D, part)
    entering = jnp.exp(-lam * nz * xf) * st[own, pl.ds(first, part), :]
    for i in range(nx):
        gap = xf - 1.0 - i
        weight = jnp.where(gap >= 0, jnp.exp(-lam * nz * jnp.maximum(gap, 0.0)), 0.0)
        entering += weight * tx[i]
    for i in range(nz):
        ss[i] = (before[i] + jnp.exp(-lam * float(i)) * entering).astype(BF)

    def s_copy(i):
        to = (z + i) % nz
        return remote(ss.at[to], sland.at[z], sa_s.at[i], sa_r.at[i], dev(x, y, to, c))

    def s_start(i, carry):
        s_copy(i).start()
        return carry

    lax.fori_loop(1, nz, s_start, 0)
    sland[z] = ss[z]

    ring(kv_copy, 2)
    ring(w_copy, 2)

    to_col = iota((depth, depth), 1)
    src_col = (to_col // rows) % nx * (nz * rows) + to_col // (nx * rows) * rows + to_col % rows
    perm[...] = jnp.where(iota((depth, depth), 0) == src_col, 1.0, 0.0).astype(BF)
    col = iota((TOK, span), 1)
    slot = col // sub
    far = (slot + 1) // 2
    least = jnp.where(slot % 2 == 1, far, nz - far)
    seen = (least <= z) | ((slot == 0) & (y * sub + col <= iota((TOK, span), 0)))
    bias[...] = jnp.where(seen, 0.0, NEG)

    def permuted(blocks):
        return dot(jnp.concatenate(blocks, axis=1).astype(BF), perm[...]).astype(BF)

    intra = []
    for h in range(H):
        cols = slice(h * D, (h + 1) * D)
        within = iota((TOK, TOK), 0) - iota((TOK, TOK), 1)
        rate = rate_of(de[h])
        inside = jnp.where(within >= 0, jnp.exp(-rate * jnp.maximum(within, 0).astype(F32)), 0.0)
        hi, lo_ = split2(dot_t(lq[:, cols], lk[:, cols]) * inside)
        intra.append(dot(hi, lv[:, cols]) + dot(lo_, lv[:, cols]))

    def s_wait(i, carry):
        s_copy(i).wait_recv()
        return carry

    lax.fori_loop(1, nz, s_wait, 0)
    ring(kv_copy, 3)
    ring(w_copy, 3)
    normed = []
    for h in range(H):
        cols = slice(h * D, (h + 1) * D)
        per = D // part
        state = jnp.concatenate([sland[h * per + k] for k in range(per)], axis=0)
        decay = jnp.exp(-rate_of(de[h]) * (iota((TOK, D), 0) + 1).astype(F32))
        normed.append(head_norm(intra[h] + dot(lq[:, cols], state) * decay, lg[:, cols]))
    ast = ag.at[2, 0, 0]
    ast[...] = permuted(normed)
    for i in range(ny):
        plane_send(ast, ag.at[0, c, x], lat_s.at[i], lat_r.at[x], i)

    for s in range(4, half + 1):
        ring(kv_copy, s)
        ring(w_copy, s)

    scale = 1.4426950408889634 / D**0.5
    for i in range(nx):
        landed(qh.at[i], qt_r.at[i])
    lane = iota((TOK, D), 1)
    packed = jnp.full((TOK, D), NEG, F32)
    for g in range(nx):

        def one_head(h, packed, g=g):
            at = pl.multiple_of(h * TOK, TOK)
            q = qh[g, pl.ds(at, TOK), :]
            scores = []
            for k in range(g + 1):
                raw = dot_t(q, kvg[0, k].reshape(span, D))
                scores.append(raw + bias[...] if k == g else raw)
            peak = jnp.full((TOK, 1), FLOOR, F32)
            for raw in scores:
                peak = jnp.maximum(peak, jnp.max(raw, axis=-1, keepdims=True))
            count = jnp.zeros((TOK, 1), F32)
            out = jnp.zeros((TOK, D), F32)
            for k, raw in enumerate(scores):
                weight = jnp.exp2((raw - peak) * scale)
                count += jnp.sum(weight, axis=-1, keepdims=True)
                out += dot(weight.astype(BF), kvg[1, k].reshape(span, D))
            some = count > 0
            safe = jnp.where(some, count, 1.0)
            osend[g, h] = (out / safe).astype(BF)
            lse = jnp.where(some, peak * scale + jnp.log2(safe), NEG)
            return jnp.where(lane == g * 8 + h, lse, packed)

        packed = lax.fori_loop(0, H, one_head, packed)
    turned = packed.T
    for g in range(nx):
        lsend[g] = turned[g * 8 : (g + 1) * 8, :]

    def o_copy(i):
        to = (y + i) % ny
        return remote(osend.at[to], oland.at[y], os_s.at[i], os_r.at[i], dev(x, to, z, c))

    def l_copy(i):
        to = (y + i) % ny
        return remote(lsend.at[to], lland.at[y], ls_s.at[i], ls_r.at[i], dev(x, to, z, c))

    for i in range(1, ny):
        l_copy(i).start()
        o_copy(i).start()
    oland[y] = osend[y]
    lland[y] = lsend[y]

    def forward(layer, block):
        ref = ag.at[layer, c, block]
        return remote(ref, ref, fw_s.at[layer, block], fw_r.at[layer, block], dev(x, y, z, 1 - c))

    for i in range(nx):
        landed(ag.at[0, 0, i], lat_r.at[i])
        forward(0, i).start()

    def c_copy(layer, i):
        to = (x + i) % nx
        return remote(
            csend.at[layer, to], cland.at[layer, x], cs_s.at[layer, i], cs_r.at[layer, i],
            dev(to, y, z, c),
        )

    def project(layer):
        w0 = wg[layer, 0].reshape(depth, NOUT)
        w1 = wg[layer, 1].reshape(depth, NOUT)
        for i in list(range(1, nx)) + [0]:
            block = (x + i) % nx
            forward(layer, block).wait_recv()
            partial = (dot(ag[layer, 0, block], w0) + dot(ag[layer, 1, block], w1)).astype(BF)
            if i == 0:
                cland[layer, x] = partial
            else:
                csend[layer, block] = partial
                c_copy(layer, i).start()

    project(0)

    for i in range(1, ny):
        l_copy(i).wait_recv()
        o_copy(i).wait_recv()
    lses = jnp.concatenate(
        [lland[j] for j in range(ny)] + [jnp.zeros((D - 8 * ny, D), F32)], axis=0
    ).T
    gains = qh[0, H * TOK :, :].astype(F32)
    gains = gains[0:4] + gains[4:8] + gains[8:12]
    normed = []
    for h in range(H):
        each = [lses[:, j * 8 + h : j * 8 + h + 1] for j in range(ny)]
        peak = functools.reduce(jnp.maximum, each)
        shares = [jnp.exp2(a - peak) for a in each]
        mixed = sum(w * oland[j, h].astype(F32) for j, w in enumerate(shares)) / sum(shares)
        normed.append(head_norm(mixed, gains[h : h + 1, :]))
    ag[1, c, y] = permuted(normed)

    def a_copy(i):
        ref = ag.at[1, c, y]
        return remote(ref, ref, sat_s.at[i], sat_r.at[i], dev(x, (y + i) % ny, z, c))

    for i in range(1, ny):
        a_copy(i).start()
    forward(1, y).start()
    for i in range(1, ny):
        a_copy(i).wait_recv()
        forward(1, (y + ny - i) % ny).start()
    project(1)

    for layer, out in ((0, lo), (1, so)):
        for i in range(1, nx):
            c_copy(layer, i).wait_recv()
        out[...] = sum(cland[layer, i].astype(F32) for i in range(nx)).astype(BF)

    for i in range(ny):
        plane_sent(kvst.at[0], kvt_s.at[i], i)
        plane_sent(wst.at[0, 0], wt_s.at[0, i], i)
        plane_sent(wst.at[0, 0], wt_s.at[1, i], i, True)
        plane_sent(qst, qt_s.at[i], i)
        plane_sent(ast, lat_s.at[i], i)

    def far_wait(i, carry):
        u_copy(i).wait_send()
        s_copy(i).wait_send()
        return carry

    lax.fori_loop(1, nz, far_wait, 0)
    for i in range(1, nx):
        tx_copy(i).wait_send()
        o_copy(i).wait_send()
        l_copy(i).wait_send()
        a_copy(i).wait_send()
        for layer in range(2):
            c_copy(layer, i).wait_send()
    for i in range(nx):
        for layer in range(2):
            forward(layer, i).wait_send()
    for stream in range(2):
        for way in range(2):
            for s in range(1, kv_steps(stream, way) + 1):
                kv_copy(stream, way, s).wait_send()
                w_copy(stream, way, s).wait_send()


def local(nx, nz, *args):
    rows = args[-1].shape[0]
    ny = nx
    half = nz // 2
    sub = TOK // ny
    depth = H * D
    part = depth // nz
    args = list(args)
    args[8] = args[8].reshape(1, depth)
    args[9] = args[9].reshape(1, depth)
    vmem = pl.BlockSpec(memory_space=pltpu.VMEM)
    specs = [vmem] * 12
    specs[4] = pl.BlockSpec(memory_space=pltpu.SMEM)
    dma = pltpu.SemaphoreType.DMA
    scratch = [
        pltpu.VMEM((ny, 2, sub, D), BF),
        pltpu.VMEM((2, nx, nz, sub, D), BF),
        pltpu.VMEM((H * TOK + 16, D), BF),
        pltpu.VMEM((nx, H * TOK + 16, D), BF),
        pltpu.VMEM((ny, 2, 2, rows, NOUT), F32),
        pltpu.VMEM((2, nx, 2, rows, NOUT), F32),
        pltpu.VMEM((2, 2, nz, nx * rows, NOUT), BF),
        pltpu.VMEM((nz, part, D), BF),
        pltpu.VMEM((nz, part, D), BF),
        pltpu.VMEM((nx, part, D), F32),
        pltpu.VMEM((nz, part, D), BF),
        pltpu.VMEM((nz, part, D), BF),
        pltpu.VMEM((nx, H, TOK, D), BF),
        pltpu.VMEM((ny, H, TOK, D), BF),
        pltpu.VMEM((nx, 8, D), F32),
        pltpu.VMEM((ny, 8, D), F32),
        pltpu.VMEM((3, 2, nx, TOK, depth), BF),
        pltpu.VMEM((2, nx, TOK, NOUT), BF),
        pltpu.VMEM((2, nx, TOK, NOUT), BF),
        pltpu.VMEM((depth, depth), BF),
        pltpu.VMEM((TOK, nz * sub), F32),
    ]
    sems = [
        (ny,), (nx,), (2, ny), (2, nx), (ny,), (nx,),
        (nz,), (nz,), (nx,), (nx,), (nz,), (nz,),
        (2, 2, half), (2, 2, half), (2, 2, half), (2, 2, half),
        (ny,), (ny,), (ny,), (ny,), (ny,), (nx,), (ny,), (ny,),
        (2, nx), (2, nx), (2, nx), (2, nx),
    ]
    out = jax.ShapeDtypeStruct((TOK, NOUT), BF)
    return pl.pallas_call(
        functools.partial(kernel, nx, nz),
        out_shape=(out, out),
        in_specs=specs,
        out_specs=(vmem, vmem),
        scratch_shapes=scratch + [dma(s) for s in sems],
        compiler_params=pltpu.CompilerParams(
            collective_id=0, has_side_effects=True, vmem_limit_bytes=48 * 1024 * 1024
        ),
        name="plane_attention",
    )(*args)


def solution(mesh):
    nx = mesh.shape["head"] // 2
    nz = mesh.shape["ctx"] // nx
    placed = (
        P("ctx", "head"),
        P("ctx", "head"),
        P("ctx", "head"),
        P("head", None, None),
        P("head"),
        P("ctx", "head"),
        P("ctx", "head"),
        P("ctx", "head"),
        P("head"),
        P("head"),
        P(("head", "ctx"), None),
        P(("head", "ctx"), None),
    )
    return jax.shard_map(
        functools.partial(local, nx, nz),
        mesh=mesh,
        in_specs=placed,
        out_specs=(P("ctx", "head"), P("ctx", "head")),
        check_vma=False,
    )
```

```python
import functools

import jax
import jax.numpy as jnp
from jax import lax
from jax.experimental import pallas as pl
from jax.experimental.pallas import tpu as pltpu
from jax.sharding import PartitionSpec as P

D = 128
H = 4
TOK = 128
NOUT = 384
MESH = pl.DeviceIdType.MESH
BF = jnp.bfloat16
F32 = jnp.float32
PARTS = 2
NEG = -1e30
FLOOR = -1e29


def dot(a, b):
    return jnp.dot(a, b, preferred_element_type=F32)


def dot_t(a, b):
    return lax.dot_general(a, b, (((1,), (1,)), ((), ())), preferred_element_type=F32)


def split2(a):
    hi = a.astype(BF)
    return hi, (a - hi.astype(F32)).astype(BF)


def iota(shape, axis):
    return lax.broadcasted_iota(jnp.int32, shape, axis)


def head_norm(values, gain):
    scale = lax.rsqrt(jnp.mean(values * values, axis=-1, keepdims=True) + 1e-06)
    return values * scale * gain


def kernel(
    nx, nz, lq_h, lk_h, lv_h, st_h, de, sq_h, sk_h, sv_h, lg_h, sg_h, lw_h, sw_h, lo, so,
    lq, lk, lv, st, lg, sg, lw, sw, in_s, kvst, kvg, qh, before, within_out, peaks, counts, acc, wst, wland, wg, us, uland, tx, ss, sland,
    osend, oland, lsend, lland, ag, csend, cland, perm, bias,
    kvt_s, kvt_r, wt_s, wt_r, qt_s, qt_r, ua_s, ua_r, tx_s, tx_r, sa_s, sa_r,
    kv_s, kv_r, wr_s, wr_r, os_s, os_r, ls_s, ls_r, at_s, at_r,
    fw_s, fw_r, cs_s, cs_r,
):
    ny = nx
    half = nz // 2
    direct = 2 if nz > 4 else 1
    rows = lw_h.shape[0]
    sub = TOK // ny
    span = nz * sub
    depth = H * D
    part = depth // nz
    ctx, head = lax.axis_index("ctx"), lax.axis_index("head")
    x, z = ctx // nz, ctx % nz
    y, c = head // 2, head % 2

    def dev(dx, dy, dz, dc):
        return (dx * nz + dz, dy * 2 + dc)

    def remote(src, dst, ssem, rsem, to):
        return pltpu.make_async_remote_copy(
            src_ref=src, dst_ref=dst, send_sem=ssem, recv_sem=rsem, device_id=to, device_id_type=MESH
        )

    on_diag = x == y

    loads = {}

    def load(name, pairs):
        loads[name] = []
        for src, dst in pairs:
            sem = in_s.at[sum(len(v) for v in loads.values())]
            loads[name].append(pltpu.make_async_copy(src, dst, sem))
            loads[name][-1].start()

    def loaded(name):
        for copy in loads[name]:
            copy.wait()

    pieces = [pl.ds(j * sub, sub) for j in range(ny)]
    load("kv", [(r.at[p], kvst.at[j, k]) for k, r in enumerate((sk_h, sv_h)) for j, p in enumerate(pieces)])
    load("w", [(lw_h, lw), (sw_h, sw)])
    load("lkv", [(lk_h, lk), (lv_h, lv)])
    load("q", [(sq_h.at[:, pl.ds(h * D, D)], qh.at[x, h]) for h in range(H)])
    load("lq", [(lq_h, lq), (lg_h, lg), (sg_h, sg), (st_h, st)])

    barrier = pltpu.get_barrier_semaphore()

    def greet(to):
        pl.semaphore_signal(barrier, inc=1, device_id=to, device_id_type=MESH)

    def greet_z(i, carry):
        greet(dev(x, y, (z + i) % nz, c))
        return carry

    lax.fori_loop(1, nz, greet_z, 0)
    for i in range(nx):
        if i > 0:
            greet(dev((x + i) % nx, y, z, c))
        greet(dev((x + i) % nx, y, z, 1 - c))
        for d in range(1, direct + 1):
            if i > 0:
                greet(dev((x + i) % nx, y, (z + d) % nz, c))
                greet(dev((x + i) % nx, y, (z + nz - d) % nz, c))
    for i in range(ny):
        if i == 0:

            @pl.when(jnp.logical_not(on_diag))
            def _():
                greet(dev(y, y, z, c))

        else:
            greet(dev(y, (y + i) % ny, z, c))

    n_greet = (nz - 1) + 3 * nx - 1 - jnp.where(on_diag, 1, 0) + 2 * direct * (nx - 1)

    def rate_of(e):
        return jnp.exp2(-jnp.full((8, D), e, jnp.int32).astype(F32))[:1]

    def landed(dst, rsem):
        pltpu.make_async_copy(dst, dst, rsem).wait()

    loaded("w")
    for layer, ref in ((0, lw), (1, sw)):
        wide = ref[...].astype(F32)
        for j in range(nx):
            for k in range(2):
                at = (j * 2 + k) * NOUT
                wst[j, k, layer] = wide[:, at : at + NOUT]
    loaded("kv")
    loaded("q")
    loaded("lkv")
    pl.semaphore_wait(barrier, n_greet)

    reach = [0] + [d * e for d in range(1, direct + 1) for e in (1, -1)]

    def slot_of(d):
        return 0 if d == 0 else 2 * d - 1 if d > 0 else -2 * d

    def kvt_copy(n, i):
        to, d = (x + i) % nx, reach[n]
        return remote(
            kvst.at[to], kvg.at[:, x, slot_of(d)], kvt_s.at[n, i], kvt_r.at[n, i],
            dev(to, y, (z + nz + d) % nz, c),
        )

    def wt_copy(k, i):
        to, core = (x + i) % nx, 1 - c if k else c
        return remote(wst.at[to, core], wland.at[c, x], wt_s.at[k, i], wt_r.at[k, i], dev(to, y, z, core))

    def along_x(ref, ssem, rsem, i):
        return remote(ref, ref, ssem.at[i], rsem.at[i], dev((x + i) % nx, y, z, c))

    def q_copy(i):
        return along_x(qh.at[x], qt_s, qt_r, i)

    far_first = sorted(range(len(reach)), key=lambda n: -abs(reach[n]))
    for n in far_first:
        for i in range(nx):
            if i > 0 or reach[n] != 0:
                kvt_copy(n, i).start()
    kvg[:, x, 0] = kvst[x]

    for h in range(H):
        rate = rate_of(de[h])
        back = (TOK - 1 - iota((TOK, D), 0)).astype(F32)
        scaled = lk[:, h * D : (h + 1) * D].astype(F32) * jnp.exp(-rate * back)
        hi, lo_ = split2(scaled.T)
        v = lv[:, h * D : (h + 1) * D]
        update = (dot(hi, v) + dot(lo_, v)).astype(BF)
        per = D // part
        for k in range(per):
            us[h * per + k] = update[k * part : (k + 1) * part, :]

    def u_copy(i):
        to = (z + i) % nz
        return remote(us.at[to], uland.at[z], ua_s.at[i], ua_r.at[i], dev(x, y, to, c))

    def u_start(i, carry):
        u_copy(i).start()
        return carry

    lax.fori_loop(1, nz, u_start, 0)
    for i in range(nx):
        for k in range(2):
            if i + k > 0:
                wt_copy(k, i).start()
    wland[c, x] = wst[x, c]
    for i in range(1, nx):
        q_copy(i).start()
    uland[z] = us[z]

    def last_step(stream, way):
        return half if stream == way else half - 1

    def kv_copy(stream, way, s):
        if way == 0:
            src, dst, to = (0 if s == 1 else 2 * s - 3), 2 * s - 1, (z + 1) % nz
        else:
            src, dst, to = 2 * s - 2, min(2 * s, nz - 1), (z + nz - 1) % nz
        return remote(
            kvg.at[stream, :, src], kvg.at[stream, :, dst],
            kv_s.at[stream, way, s - 1], kv_r.at[stream, way, s - 1], dev(x, y, to, c),
        )

    def w_copy(stream, way, s):
        if way == 0:
            at, to = (z + nz - s + 1) % nz, (z + 1) % nz
        else:
            at, to = (z + s - 1) % nz, (z + nz - 1) % nz
        block = wg.at[stream, :, at]
        return remote(
            block, block, wr_s.at[stream, way, s - 1], wr_r.at[stream, way, s - 1], dev(x, y, to, c)
        )

    def ring(copy, s, begin=False):
        for stream in range(2):
            for way in range(2):
                if not begin and s <= last_step(stream, way):
                    copy(stream, way, s).wait_recv()
                if s + 1 <= last_step(stream, way):
                    copy(stream, way, s + 1).start()

    for n in far_first:
        for i in range(nx):
            if i > 0 or reach[n] != 0:
                kvt_copy(n, i).wait_recv()
        if n == 2 * direct:
            ring(kv_copy, direct, True)

    for i in range(nx):
        for k in range(2):
            if i + k > 0:
                wt_copy(k, i).wait_recv()
    for layer in range(2):
        for k in range(2):
            slab = jnp.concatenate([wland[k, i, layer] for i in range(nx)], axis=0)
            wg[layer, k, z] = slab.astype(BF)
    ring(w_copy, 0, True)

    to_col = iota((depth, depth), 1)
    src_col = (to_col // rows) % nx * (nz * rows) + to_col // (nx * rows) * rows + to_col % rows
    perm[...] = jnp.where(iota((depth, depth), 0) == src_col, 1.0, 0.0).astype(BF)
    col = iota((TOK, span), 1)
    slot = col // sub
    far = (slot + 1) // 2
    least = jnp.where(slot % 2 == 1, far, nz - far)
    seen = (least <= z) | ((slot == 0) & (x * sub + col <= iota((TOK, span), 0)))
    bias[...] = jnp.where(seen, 0.0, NEG)

    def permuted(blocks):
        return dot(jnp.concatenate(blocks, axis=1).astype(BF), perm[...]).astype(BF)

    loaded("lq")
    for h in range(H):
        cols = slice(h * D, (h + 1) * D)
        within = iota((TOK, TOK), 0) - iota((TOK, TOK), 1)
        rate = rate_of(de[h])
        inside = jnp.where(within >= 0, jnp.exp(-rate * jnp.maximum(within, 0).astype(F32)), 0.0)
        hi, lo_ = split2(dot_t(lq[:, cols], lk[:, cols]) * inside)
        within_out[h] = dot(hi, lv[:, cols]) + dot(lo_, lv[:, cols])

    def tx_copy(i):
        return along_x(tx.at[x], tx_s, tx_r, i)

    own = z * part // D
    lam = rate_of(de[own]) * float(TOK)

    def state_rows():
        def u_wait(i, carry):
            u_copy(i).wait_recv()
            return carry

        lax.fori_loop(1, nz, u_wait, 0)
        step = jnp.exp(-lam)
        total = jnp.zeros((part, D), F32)
        for i in range(nz):
            before[i] = total
            total = step * total + uland[i].astype(F32)
        tx[x] = total
        for i in range(1, nx):
            tx_copy(i).start()

    def s_copy(i):
        to = (z + i) % nz
        return remote(ss.at[to], sland.at[z], sa_s.at[i], sa_r.at[i], dev(x, y, to, c))

    def state_back():
        for i in range(1, nx):
            tx_copy(i).wait_recv()
        xf = jnp.full((8, D), x, jnp.int32).astype(F32)[:1]
        first = pl.multiple_of((z * part) % D, part)
        entering = jnp.exp(-lam * nz * xf) * st[own, pl.ds(first, part), :]
        for i in range(nx):
            gap = xf - 1.0 - i
            weight = jnp.where(gap >= 0, jnp.exp(-lam * nz * jnp.maximum(gap, 0.0)), 0.0)
            entering += weight * tx[i]
        for i in range(nz):
            ss[i] = (before[i] + jnp.exp(-lam * float(i)) * entering).astype(BF)

        def s_start(i, carry):
            s_copy(i).start()
            return carry

        lax.fori_loop(1, nz, s_start, 0)
        sland[z] = ss[z]

    some_tok = TOK // PARTS

    def tokens(p):
        return pl.ds(p * some_tok, some_tok)

    def a_copy(layer, i, p):
        return along_x(ag.at[layer, c, x, tokens(p)], at_s.at[layer, p], at_r.at[layer, p], i)

    def forward(layer, block, p):
        ref = ag.at[layer, c, block, tokens(p)]
        return remote(ref, ref, fw_s.at[layer, p, block], fw_r.at[layer, p, block], dev(x, y, z, 1 - c))

    def spread(layer, p):
        for i in range(1, nx):
            a_copy(layer, i, p).start()
        forward(layer, x, p).start()

    def passed_on(layer, p):
        for i in range(1, nx):
            a_copy(layer, i, p).wait_recv()
            forward(layer, (x + nx - i) % nx, p).start()

    def lightning_out():
        def s_wait(i, carry):
            s_copy(i).wait_recv()
            return carry

        lax.fori_loop(1, nz, s_wait, 0)
        normed = []
        for h in range(H):
            cols = slice(h * D, (h + 1) * D)
            per = D // part
            state = jnp.concatenate([sland[h * per + k] for k in range(per)], axis=0)
            decay = jnp.exp(-rate_of(de[h]) * (iota((TOK, D), 0) + 1).astype(F32))
            out = within_out[h] + dot(lq[:, cols], state) * decay
            normed.append(head_norm(out, lg[:, cols]))
        ag[0, c, x] = permuted(normed)
        for p in range(PARTS):
            spread(0, p)

    scale = 1.4426950408889634 / D**0.5
    lane = iota((TOK, D), 1)
    cut = nz - 4 if nz > 4 else 2
    bounds = (0, cut, nz)

    def o_copy(i, p):
        to = (x + i) % nx
        return remote(osend.at[to, p], oland.at[x, p], os_s.at[p, i], os_r.at[p, i], dev(to, y, z, c))

    def l_copy(i):
        to = (x + i) % nx
        return remote(lsend.at[to], lland.at[x], ls_s.at[i], ls_r.at[i], dev(to, y, z, c))

    def attend(g, chunk):
        keys = slice(bounds[chunk], bounds[chunk + 1])
        width = (bounds[chunk + 1] - bounds[chunk]) * sub
        cols = slice(bounds[chunk] * sub, bounds[chunk + 1] * sub)

        q = qh[g].reshape(depth, D)
        if chunk == 0:
            old = jnp.full((depth, 1), FLOOR, F32)
        else:
            old = peaks[g][:, :1]
        scores = []
        peak = old
        for k in range(g + 1):
            raw = dot_t(q, kvg[0, k, keys].reshape(width, D))
            if k == g:
                mask = bias[:, cols]
                raw = (raw.reshape(H, TOK, width) + mask[None]).reshape(depth, width)
            peak = jnp.maximum(peak, jnp.max(raw, axis=-1, keepdims=True))
            scores.append(raw)
        if chunk == 0:
            count = jnp.zeros((depth, 1), F32)
            out = jnp.zeros((depth, D), F32)
        else:
            fade = jnp.exp2((old - peak) * scale)
            count = counts[g][:, :1] * fade
            out = acc[g] * fade
        for k, raw in enumerate(scores):
            weight = jnp.exp2((raw - peak) * scale)
            count += jnp.sum(weight, axis=-1, keepdims=True)
            out += dot(weight.astype(BF), kvg[1, k, keys].reshape(width, D))
        if chunk == 0:
            peaks[g] = jnp.broadcast_to(peak, (depth, D))
            counts[g] = jnp.broadcast_to(count, (depth, D))
            acc[g] = out
            return
        some = count > 0
        safe = jnp.where(some, count, 1.0)
        out = (out / safe).astype(BF).reshape(H, TOK, D)
        for p in range(PARTS):
            osend[g, p] = out[:, p * some_tok : (p + 1) * some_tok]
        lse = jnp.where(some, peak * scale + jnp.log2(safe), NEG)
        packed = jnp.full((TOK, D), NEG, F32)
        for h in range(H):
            packed = jnp.where(lane == h, lse[h * TOK : (h + 1) * TOK], packed)
        lsend[g] = packed.T[:8, :]

    def outputs_out():
        for i in range(1, nx):
            l_copy(i).start()
        for p in range(PARTS):
            for i in range(1, nx):
                o_copy(i, p).start()
        oland[x] = osend[x]
        lland[x] = lsend[x]

    def c_copy(layer, i, p):
        to = (x + i) % nx
        return remote(
            csend.at[layer, to, tokens(p)], cland.at[layer, y, tokens(p)],
            cs_s.at[layer, p, i], cs_r.at[layer, p, y], dev(to, x, z, c),
        )

    def project(layer, parts):
        for p in parts:
            for i in range(nx):
                forward(layer, i, p).wait_recv()
        low, tall = parts[0] * some_tok, len(parts) * some_tok
        at = pl.ds(low, tall)
        partial = sum(
            dot(ag[layer, k, :, at].reshape(nx * tall, depth), wg[layer, k].reshape(depth, NOUT))
            for k in range(2)
        )
        csend[layer, :, at] = partial.astype(BF).reshape(nx, tall, NOUT)
        for p in parts:
            for i in range(1, nx):
                c_copy(layer, i, p).start()

            @pl.when(on_diag)
            def _(p=p):
                cland[layer, y, tokens(p)] = csend[layer, x, tokens(p)]

            @pl.when(jnp.logical_not(on_diag))
            def _(p=p):
                c_copy(layer, 0, p).start()

    def share_logs():
        for i in range(1, nx):
            l_copy(i).wait_recv()
        packed = [lland[j] for j in range(nx)] + [jnp.zeros((D - 8 * nx, D), F32)]
        return jnp.concatenate(packed, axis=0).T

    def combine(lses, p):
        for i in range(1, nx):
            o_copy(i, p).wait_recv()
        lses = lses[p * some_tok : (p + 1) * some_tok]
        normed = []
        for h in range(H):
            each = [lses[:, j * 8 + h : j * 8 + h + 1] for j in range(nx)]
            peak = functools.reduce(jnp.maximum, each)
            shares = [jnp.exp2(a - peak) for a in each]
            mixed = sum(w * oland[j, p, h].astype(F32) for j, w in enumerate(shares)) / sum(shares)
            normed.append(head_norm(mixed, sg[:, h * D : (h + 1) * D]))
        ag[1, c, x, tokens(p)] = permuted(normed)

    kv_next, w_next = [direct + 1], [1]

    def kv_step():
        if kv_next[0] <= half:
            ring(kv_copy, kv_next[0])
            kv_next[0] += 1

    def w_step():
        if w_next[0] <= half:
            ring(w_copy, w_next[0])
            w_next[0] += 1

    kv_step()
    w_step()
    kv_step()
    w_step()
    state_rows()
    kv_step()
    w_step()
    state_back()
    for i in range(1, nx):
        q_copy(i).wait_recv()
    kv_step()
    w_step()
    attend(nx - 1, 0)
    kv_step()
    w_step()
    for g in range(nx - 2, -1, -1):
        attend(g, 0)
    while kv_next[0] <= half:
        kv_step()
    lightning_out()
    for g in range(nx - 1, -1, -1):
        attend(g, 1)
    outputs_out()
    w_step()
    w_step()
    lses = share_logs()
    for p in range(PARTS):
        combine(lses, p)
        spread(1, p)
    while w_next[0] <= half:
        w_step()
    for p in range(PARTS):
        passed_on(0, p)
    project(0, range(PARTS))
    for p in range(PARTS):
        passed_on(1, p)
        project(1, [p])

    for layer, out in ((0, lo), (1, so)):
        for p in range(PARTS):
            for i in range(1, ny):
                src = (y + i) % ny
                landed(cland.at[layer, src, tokens(p)], cs_r.at[layer, p, src])

            @pl.when(jnp.logical_not(on_diag))
            def _(layer=layer, p=p):
                landed(cland.at[layer, y, tokens(p)], cs_r.at[layer, p, y])

        out[...] = sum(cland[layer, i].astype(F32) for i in range(ny)).astype(BF)

    for n in far_first:
        for i in range(nx):
            if i > 0 or reach[n] != 0:
                kvt_copy(n, i).wait_send()
    for i in range(nx):
        for k in range(2):
            if i + k > 0:
                wt_copy(k, i).wait_send()
    def far_wait(i, carry):
        u_copy(i).wait_send()
        s_copy(i).wait_send()
        return carry

    lax.fori_loop(1, nz, far_wait, 0)
    for i in range(1, nx):
        tx_copy(i).wait_send()
        q_copy(i).wait_send()
        l_copy(i).wait_send()
        for p in range(PARTS):
            o_copy(i, p).wait_send()
            for layer in range(2):
                a_copy(layer, i, p).wait_send()
                c_copy(layer, i, p).wait_send()

    @pl.when(jnp.logical_not(on_diag))
    def _():
        for layer in range(2):
            for p in range(PARTS):
                c_copy(layer, 0, p).wait_send()

    for i in range(nx):
        for layer in range(2):
            for p in range(PARTS):
                forward(layer, i, p).wait_send()
    for stream in range(2):
        for way in range(2):
            for s in range(1, last_step(stream, way) + 1):
                if s > direct:
                    kv_copy(stream, way, s).wait_send()
                w_copy(stream, way, s).wait_send()


def local(nx, nz, *args):
    rows = args[-1].shape[0]
    ny = nx
    half = nz // 2
    sub = TOK // ny
    depth = H * D
    part = depth // nz
    args = list(args)
    args[8] = args[8].reshape(1, depth)
    args[9] = args[9].reshape(1, depth)
    vmem = pl.BlockSpec(memory_space=pltpu.VMEM)
    specs = [pl.BlockSpec(memory_space=pltpu.HBM)] * 12
    specs[4] = pl.BlockSpec(memory_space=pltpu.SMEM)
    dma = pltpu.SemaphoreType.DMA
    scratch = [
        pltpu.VMEM((TOK, depth), BF),
        pltpu.VMEM((TOK, depth), BF),
        pltpu.VMEM((TOK, depth), BF),
        pltpu.VMEM((H, D, D), F32),
        pltpu.VMEM((1, depth), F32),
        pltpu.VMEM((1, depth), F32),
        pltpu.VMEM((rows, args[10].shape[1]), BF),
        pltpu.VMEM((rows, args[10].shape[1]), BF),
        dma((2 * ny + H + 8,)),
        pltpu.VMEM((ny, 2, sub, D), BF),
        pltpu.VMEM((2, nx, nz, sub, D), BF),
        pltpu.VMEM((nx, H, TOK, D), BF),
        pltpu.VMEM((nz, part, D), F32),
        pltpu.VMEM((H, TOK, D), F32),
        pltpu.VMEM((nx, depth, D), F32),
        pltpu.VMEM((nx, depth, D), F32),
        pltpu.VMEM((nx, depth, D), F32),
        pltpu.VMEM((ny, 2, 2, rows, NOUT), F32),
        pltpu.VMEM((2, nx, 2, rows, NOUT), F32),
        pltpu.VMEM((2, 2, nz, nx * rows, NOUT), BF),
        pltpu.VMEM((nz, part, D), BF),
        pltpu.VMEM((nz, part, D), BF),
        pltpu.VMEM((nx, part, D), F32),
        pltpu.VMEM((nz, part, D), BF),
        pltpu.VMEM((nz, part, D), BF),
        pltpu.VMEM((nx, PARTS, H, TOK // PARTS, D), BF),
        pltpu.VMEM((nx, PARTS, H, TOK // PARTS, D), BF),
        pltpu.VMEM((nx, 8, D), F32),
        pltpu.VMEM((ny, 8, D), F32),
        pltpu.VMEM((2, 2, nx, TOK, depth), BF),
        pltpu.VMEM((2, nx, TOK, NOUT), BF),
        pltpu.VMEM((2, nx, TOK, NOUT), BF),
        pltpu.VMEM((depth, depth), BF),
        pltpu.VMEM((TOK, nz * sub), F32),
    ]
    sems = [
        (5, nx), (5, nx), (2, nx), (2, nx), (nx,), (nx,),
        (nz,), (nz,), (nx,), (nx,), (nz,), (nz,),
        (2, 2, half), (2, 2, half), (2, 2, half), (2, 2, half),
        (PARTS, nx), (PARTS, nx), (nx,), (nx,), (2, PARTS, nx), (2, PARTS, nx),
        (2, PARTS, nx), (2, PARTS, nx), (2, PARTS, nx), (2, PARTS, nx),
    ]
    out = jax.ShapeDtypeStruct((TOK, NOUT), BF)
    return pl.pallas_call(
        functools.partial(kernel, nx, nz),
        out_shape=(out, out),
        in_specs=specs,
        out_specs=(vmem, vmem),
        scratch_shapes=scratch + [dma(s) for s in sems],
        compiler_params=pltpu.CompilerParams(
            collective_id=0, has_side_effects=True, vmem_limit_bytes=62 * 1024 * 1024
        ),
        name="plane_attention",
    )(*args)


def solution(mesh):
    nx = mesh.shape["head"] // 2
    nz = mesh.shape["ctx"] // nx
    placed = (
        P("ctx", "head"),
        P("ctx", "head"),
        P("ctx", "head"),
        P("head", None, None),
        P("head"),
        P("ctx", "head"),
        P("ctx", "head"),
        P("ctx", "head"),
        P("head"),
        P("head"),
        P(("head", "ctx"), None),
        P(("head", "ctx"), None),
    )
    return jax.shard_map(
        functools.partial(local, nx, nz),
        mesh=mesh,
        in_specs=placed,
        out_specs=(P("ctx", "head"), P("ctx", "head")),
        check_vma=False,
    )
```

```python
import functools

import jax
import jax.numpy as jnp
from jax import lax
from jax.experimental import pallas as pl
from jax.experimental.pallas import tpu as pltpu
from jax.sharding import PartitionSpec as P

D = 128
H = 4
TOK = 128
NOUT = 384
MESH = pl.DeviceIdType.MESH
BF = jnp.bfloat16
F32 = jnp.float32
PARTS = 2
NEG = -1e30
FLOOR = -1e29


def dot(a, b):
    return jnp.dot(a, b, preferred_element_type=F32)


def dot_t(a, b):
    return lax.dot_general(a, b, (((1,), (1,)), ((), ())), preferred_element_type=F32)


def split2(a):
    hi = a.astype(BF)
    return hi, (a - hi.astype(F32)).astype(BF)


def iota(shape, axis):
    return lax.broadcasted_iota(jnp.int32, shape, axis)


def head_norm(values, gain):
    scale = lax.rsqrt(jnp.mean(values * values, axis=-1, keepdims=True) + 1e-06)
    return values * scale * gain


def kernel(
    nx, nz, lq_h, lk_h, lv_h, st_h, de, sq_h, sk_h, sv_h, lg_h, sg_h, lw_h, sw_h, lo, so,
    lq, lk, lv, st, lg, sg, lw, sw, in_s, kvst, kvg, qh, before, within_out, peaks, counts, acc, wst, wland, wg, us, uland, tx, ss, sland,
    osend, oland, lsend, lland, ag, csend, cland, perm, bias,
    kvt_s, kvt_r, wt_s, wt_r, qt_s, qt_r, ua_s, ua_r, tx_s, tx_r, sa_s, sa_r,
    kv_s, kv_r, wr_s, wr_r, os_s, os_r, ls_s, ls_r, at_s, at_r,
    fw_s, fw_r, cs_s, cs_r,
):
    ny = nx
    half = nz // 2
    direct = 2 if nz > 4 else 1
    rows = lw_h.shape[0]
    sub = TOK // ny
    span = nz * sub
    depth = H * D
    part = depth // nz
    ctx, head = lax.axis_index("ctx"), lax.axis_index("head")
    x, z = ctx // nz, ctx % nz
    y, c = head // 2, head % 2

    def dev(dx, dy, dz, dc):
        return (dx * nz + dz, dy * 2 + dc)

    def remote(src, dst, ssem, rsem, to):
        return pltpu.make_async_remote_copy(
            src_ref=src, dst_ref=dst, send_sem=ssem, recv_sem=rsem, device_id=to, device_id_type=MESH
        )

    on_diag = x == y

    loads = {}

    def load(name, pairs):
        loads[name] = []
        for src, dst in pairs:
            sem = in_s.at[sum(len(v) for v in loads.values())]
            loads[name].append(pltpu.make_async_copy(src, dst, sem))
            loads[name][-1].start()

    def loaded(name):
        for copy in loads[name]:
            copy.wait()

    pieces = [pl.ds(j * sub, sub) for j in range(ny)]
    load("kv", [(r.at[p], kvst.at[j, k]) for k, r in enumerate((sk_h, sv_h)) for j, p in enumerate(pieces)])
    load("w", [(lw_h, lw), (sw_h, sw)])
    load("lkv", [(lk_h, lk), (lv_h, lv)])
    load("q", [(sq_h.at[:, pl.ds(h * D, D)], qh.at[x, h]) for h in range(H)])
    load("lq", [(lq_h, lq), (lg_h, lg), (sg_h, sg), (st_h, st)])

    barrier = pltpu.get_barrier_semaphore()

    def greet(to):
        pl.semaphore_signal(barrier, inc=1, device_id=to, device_id_type=MESH)

    def greet_z(i, carry):
        greet(dev(x, y, (z + i) % nz, c))
        return carry

    lax.fori_loop(1, nz, greet_z, 0)
    for i in range(nx):
        if i > 0:
            greet(dev((x + i) % nx, y, z, c))
        greet(dev((x + i) % nx, y, z, 1 - c))
        for d in range(1, direct + 1):
            if i > 0:
                greet(dev((x + i) % nx, y, (z + d) % nz, c))
                greet(dev((x + i) % nx, y, (z + nz - d) % nz, c))
    for i in range(ny):
        if i == 0:

            @pl.when(jnp.logical_not(on_diag))
            def _():
                greet(dev(y, y, z, c))

        else:
            greet(dev(y, (y + i) % ny, z, c))

    n_greet = (nz - 1) + 3 * nx - 1 - jnp.where(on_diag, 1, 0) + 2 * direct * (nx - 1)

    def rate_of(e):
        return jnp.exp2(-jnp.full((8, D), e, jnp.int32).astype(F32))[:1]

    def landed(dst, rsem):
        pltpu.make_async_copy(dst, dst, rsem).wait()

    loaded("w")
    for layer, ref in ((0, lw), (1, sw)):
        wide = ref[...].astype(F32)
        for j in range(nx):
            for k in range(2):
                at = (j * 2 + k) * NOUT
                wst[j, k, layer] = wide[:, at : at + NOUT]
    loaded("kv")
    loaded("q")
    loaded("lkv")
    for h in range(H):
        rate = rate_of(de[h])
        back = (TOK - 1 - iota((TOK, D), 0)).astype(F32)
        scaled = lk[:, h * D : (h + 1) * D].astype(F32) * jnp.exp(-rate * back)
        hi, lo_ = split2(scaled.T)
        v = lv[:, h * D : (h + 1) * D]
        update = (dot(hi, v) + dot(lo_, v)).astype(BF)
        per = D // part
        for k in range(per):
            us[h * per + k] = update[k * part : (k + 1) * part, :]

    to_col = iota((depth, depth), 1)
    src_col = (to_col // rows) % nx * (nz * rows) + to_col // (nx * rows) * rows + to_col % rows
    perm[...] = jnp.where(iota((depth, depth), 0) == src_col, 1.0, 0.0).astype(BF)
    col = iota((TOK, span), 1)
    slot = col // sub
    far = (slot + 1) // 2
    least = jnp.where(slot % 2 == 1, far, nz - far)
    seen = (least <= z) | ((slot == 0) & (x * sub + col <= iota((TOK, span), 0)))
    bias[...] = jnp.where(seen, 0.0, NEG)

    def permuted(blocks):
        return dot(jnp.concatenate(blocks, axis=1).astype(BF), perm[...]).astype(BF)

    loaded("lq")
    for h in range(H):
        cols = slice(h * D, (h + 1) * D)
        within = iota((TOK, TOK), 0) - iota((TOK, TOK), 1)
        rate = rate_of(de[h])
        inside = jnp.where(within >= 0, jnp.exp(-rate * jnp.maximum(within, 0).astype(F32)), 0.0)
        hi, lo_ = split2(dot_t(lq[:, cols], lk[:, cols]) * inside)
        within_out[h] = dot(hi, lv[:, cols]) + dot(lo_, lv[:, cols])

    pl.semaphore_wait(barrier, n_greet)

    reach = [0] + [d * e for d in range(1, direct + 1) for e in (1, -1)]

    def slot_of(d):
        return 0 if d == 0 else 2 * d - 1 if d > 0 else -2 * d

    def kvt_copy(n, i):
        to, d = (x + i) % nx, reach[n]
        return remote(
            kvst.at[to], kvg.at[:, x, slot_of(d)], kvt_s.at[n, i], kvt_r.at[n, i],
            dev(to, y, (z + nz + d) % nz, c),
        )

    def wt_copy(k, i):
        to, core = (x + i) % nx, 1 - c if k else c
        return remote(wst.at[to, core], wland.at[c, x], wt_s.at[k, i], wt_r.at[k, i], dev(to, y, z, core))

    def along_x(ref, ssem, rsem, i):
        return remote(ref, ref, ssem.at[i], rsem.at[i], dev((x + i) % nx, y, z, c))

    def q_copy(i):
        return along_x(qh.at[x], qt_s, qt_r, i)

    far_first = sorted(range(len(reach)), key=lambda n: -abs(reach[n]))
    for n in far_first:
        for i in range(nx):
            if i > 0 or reach[n] != 0:
                kvt_copy(n, i).start()
    kvg[:, x, 0] = kvst[x]

    for i in range(nx):
        for k in range(2):
            if i + k > 0:
                wt_copy(k, i).start()
    wland[c, x] = wst[x, c]
    def u_copy(i):
        to = (z + i) % nz
        return remote(us.at[to], uland.at[z], ua_s.at[i], ua_r.at[i], dev(x, y, to, c))

    def u_start(i, carry):
        u_copy(i).start()
        return carry

    lax.fori_loop(1, nz, u_start, 0)
    for i in range(1, nx):
        q_copy(i).start()
    uland[z] = us[z]

    def last_step(stream, way):
        return half if stream == way else half - 1

    def kv_copy(stream, way, s):
        if way == 0:
            src, dst, to = (0 if s == 1 else 2 * s - 3), 2 * s - 1, (z + 1) % nz
        else:
            src, dst, to = 2 * s - 2, min(2 * s, nz - 1), (z + nz - 1) % nz
        return remote(
            kvg.at[stream, :, src], kvg.at[stream, :, dst],
            kv_s.at[stream, way, s - 1], kv_r.at[stream, way, s - 1], dev(x, y, to, c),
        )

    def w_copy(stream, way, s):
        if way == 0:
            at, to = (z + nz - s + 1) % nz, (z + 1) % nz
        else:
            at, to = (z + s - 1) % nz, (z + nz - 1) % nz
        block = wg.at[stream, :, at]
        return remote(
            block, block, wr_s.at[stream, way, s - 1], wr_r.at[stream, way, s - 1], dev(x, y, to, c)
        )

    def ring(copy, s, begin=False):
        for stream in range(2):
            for way in range(2):
                if not begin and s <= last_step(stream, way):
                    copy(stream, way, s).wait_recv()
                if s + 1 <= last_step(stream, way):
                    copy(stream, way, s + 1).start()

    for n in far_first:
        for i in range(nx):
            if i > 0 or reach[n] != 0:
                kvt_copy(n, i).wait_recv()
        if n == 2 * direct:
            ring(kv_copy, direct, True)

    for i in range(nx):
        for k in range(2):
            if i + k > 0:
                wt_copy(k, i).wait_recv()
    for layer in range(2):
        for k in range(2):
            slab = jnp.concatenate([wland[k, i, layer] for i in range(nx)], axis=0)
            wg[layer, k, z] = slab.astype(BF)
    ring(w_copy, 0, True)

    def tx_copy(i):
        return along_x(tx.at[x], tx_s, tx_r, i)

    own = z * part // D
    lam = rate_of(de[own]) * float(TOK)

    def state_rows():
        def u_wait(i, carry):
            u_copy(i).wait_recv()
            return carry

        lax.fori_loop(1, nz, u_wait, 0)
        step = jnp.exp(-lam)
        total = jnp.zeros((part, D), F32)
        for i in range(nz):
            before[i] = total
            total = step * total + uland[i].astype(F32)
        tx[x] = total
        for i in range(1, nx):
            tx_copy(i).start()

    def s_copy(i):
        to = (z + i) % nz
        return remote(ss.at[to], sland.at[z], sa_s.at[i], sa_r.at[i], dev(x, y, to, c))

    def state_back():
        for i in range(1, nx):
            tx_copy(i).wait_recv()
        xf = jnp.full((8, D), x, jnp.int32).astype(F32)[:1]
        first = pl.multiple_of((z * part) % D, part)
        entering = jnp.exp(-lam * nz * xf) * st[own, pl.ds(first, part), :]
        for i in range(nx):
            gap = xf - 1.0 - i
            weight = jnp.where(gap >= 0, jnp.exp(-lam * nz * jnp.maximum(gap, 0.0)), 0.0)
            entering += weight * tx[i]
        for i in range(nz):
            ss[i] = (before[i] + jnp.exp(-lam * float(i)) * entering).astype(BF)

        def s_start(i, carry):
            s_copy(i).start()
            return carry

        lax.fori_loop(1, nz, s_start, 0)
        sland[z] = ss[z]

    some_tok = TOK // PARTS

    def tokens(p):
        return pl.ds(p * some_tok, some_tok)

    def a_copy(layer, i, p):
        return along_x(ag.at[layer, c, x, tokens(p)], at_s.at[layer, p], at_r.at[layer, p], i)

    def forward(layer, block, p):
        ref = ag.at[layer, c, block, tokens(p)]
        return remote(ref, ref, fw_s.at[layer, p, block], fw_r.at[layer, p, block], dev(x, y, z, 1 - c))

    def spread(layer, p):
        for i in range(1, nx):
            a_copy(layer, i, p).start()
        forward(layer, x, p).start()

    def passed_on(layer, p):
        for i in range(1, nx):
            a_copy(layer, i, p).wait_recv()
            forward(layer, (x + nx - i) % nx, p).start()

    def lightning_out():
        def s_wait(i, carry):
            s_copy(i).wait_recv()
            return carry

        lax.fori_loop(1, nz, s_wait, 0)
        normed = []
        for h in range(H):
            cols = slice(h * D, (h + 1) * D)
            per = D // part
            state = jnp.concatenate([sland[h * per + k] for k in range(per)], axis=0)
            decay = jnp.exp(-rate_of(de[h]) * (iota((TOK, D), 0) + 1).astype(F32))
            out = within_out[h] + dot(lq[:, cols], state) * decay
            normed.append(head_norm(out, lg[:, cols]))
        ag[0, c, x] = permuted(normed)
        for p in range(PARTS):
            spread(0, p)

    scale = 1.4426950408889634 / D**0.5
    lane = iota((TOK, D), 1)
    cut = nz - 4 if nz > 4 else 2
    bounds = (0, cut, nz)

    def o_copy(i, p):
        to = (x + i) % nx
        return remote(osend.at[to, p], oland.at[x, p], os_s.at[p, i], os_r.at[p, i], dev(to, y, z, c))

    def l_copy(i):
        to = (x + i) % nx
        return remote(lsend.at[to], lland.at[x], ls_s.at[i], ls_r.at[i], dev(to, y, z, c))

    def attend(g, chunk):
        keys = slice(bounds[chunk], bounds[chunk + 1])
        width = (bounds[chunk + 1] - bounds[chunk]) * sub
        cols = slice(bounds[chunk] * sub, bounds[chunk + 1] * sub)

        q = qh[g].reshape(depth, D)
        if chunk == 0:
            old = jnp.full((depth, 1), FLOOR, F32)
        else:
            old = peaks[g][:, :1]
        scores = []
        peak = old
        for k in range(g + 1):
            raw = dot_t(q, kvg[0, k, keys].reshape(width, D))
            if k == g:
                mask = bias[:, cols]
                raw = (raw.reshape(H, TOK, width) + mask[None]).reshape(depth, width)
            peak = jnp.maximum(peak, jnp.max(raw, axis=-1, keepdims=True))
            scores.append(raw)
        if chunk == 0:
            count = jnp.zeros((depth, 1), F32)
            out = jnp.zeros((depth, D), F32)
        else:
            fade = jnp.exp2((old - peak) * scale)
            count = counts[g][:, :1] * fade
            out = acc[g] * fade
        for k, raw in enumerate(scores):
            weight = jnp.exp2((raw - peak) * scale)
            count += jnp.sum(weight, axis=-1, keepdims=True)
            out += dot(weight.astype(BF), kvg[1, k, keys].reshape(width, D))
        if chunk == 0:
            peaks[g] = jnp.broadcast_to(peak, (depth, D))
            counts[g] = jnp.broadcast_to(count, (depth, D))
            acc[g] = out
            return
        some = count > 0
        safe = jnp.where(some, count, 1.0)
        out = (out / safe).astype(BF).reshape(H, TOK, D)
        for p in range(PARTS):
            osend[g, p] = out[:, p * some_tok : (p + 1) * some_tok]
        lse = jnp.where(some, peak * scale + jnp.log2(safe), NEG)
        packed = jnp.full((TOK, D), NEG, F32)
        for h in range(H):
            packed = jnp.where(lane == h, lse[h * TOK : (h + 1) * TOK], packed)
        lsend[g] = packed.T[:8, :]

    def outputs_out():
        for i in range(1, nx):
            l_copy(i).start()
        for p in range(PARTS):
            for i in range(1, nx):
                o_copy(i, p).start()
        oland[x] = osend[x]
        lland[x] = lsend[x]

    def c_copy(layer, i, p):
        to = (x + i) % nx
        return remote(
            csend.at[layer, to, tokens(p)], cland.at[layer, y, tokens(p)],
            cs_s.at[layer, p, i], cs_r.at[layer, p, y], dev(to, x, z, c),
        )

    def project(layer, parts):
        for p in parts:
            for i in range(nx):
                forward(layer, i, p).wait_recv()
        low, tall = parts[0] * some_tok, len(parts) * some_tok
        at = pl.ds(low, tall)
        partial = sum(
            dot(ag[layer, k, :, at].reshape(nx * tall, depth), wg[layer, k].reshape(depth, NOUT))
            for k in range(2)
        )
        csend[layer, :, at] = partial.astype(BF).reshape(nx, tall, NOUT)
        for p in parts:
            for i in range(1, nx):
                c_copy(layer, i, p).start()

            @pl.when(on_diag)
            def _(p=p):
                cland[layer, y, tokens(p)] = csend[layer, x, tokens(p)]

            @pl.when(jnp.logical_not(on_diag))
            def _(p=p):
                c_copy(layer, 0, p).start()

    def share_logs():
        for i in range(1, nx):
            l_copy(i).wait_recv()
        packed = [lland[j] for j in range(nx)] + [jnp.zeros((D - 8 * nx, D), F32)]
        return jnp.concatenate(packed, axis=0).T

    def combine(lses, p):
        for i in range(1, nx):
            o_copy(i, p).wait_recv()
        lses = lses[p * some_tok : (p + 1) * some_tok]
        normed = []
        for h in range(H):
            each = [lses[:, j * 8 + h : j * 8 + h + 1] for j in range(nx)]
            peak = functools.reduce(jnp.maximum, each)
            shares = [jnp.exp2(a - peak) for a in each]
            mixed = sum(w * oland[j, p, h].astype(F32) for j, w in enumerate(shares)) / sum(shares)
            normed.append(head_norm(mixed, sg[:, h * D : (h + 1) * D]))
        ag[1, c, x, tokens(p)] = permuted(normed)

    kv_next, w_next = [direct + 1], [1]

    def kv_step():
        if kv_next[0] <= half:
            ring(kv_copy, kv_next[0])
            kv_next[0] += 1

    def w_step():
        if w_next[0] <= half:
            ring(w_copy, w_next[0])
            w_next[0] += 1

    kv_step()
    w_step()
    kv_step()
    w_step()
    state_rows()
    kv_step()
    w_step()
    state_back()
    for i in range(1, nx):
        q_copy(i).wait_recv()
    kv_step()
    w_step()
    attend(nx - 1, 0)
    kv_step()
    w_step()
    for g in range(nx - 2, -1, -1):
        attend(g, 0)
    while kv_next[0] <= half:
        kv_step()
    lightning_out()
    for g in range(nx - 1, -1, -1):
        attend(g, 1)
    outputs_out()
    w_step()
    w_step()
    lses = share_logs()
    for p in range(PARTS):
        combine(lses, p)
        spread(1, p)
    while w_next[0] <= half:
        w_step()
    for p in range(PARTS):
        passed_on(0, p)
    project(0, range(PARTS))
    for p in range(PARTS):
        passed_on(1, p)
        project(1, [p])

    for n in far_first:
        for i in range(nx):
            if i > 0 or reach[n] != 0:
                kvt_copy(n, i).wait_send()
    for i in range(nx):
        for k in range(2):
            if i + k > 0:
                wt_copy(k, i).wait_send()
    def far_wait(i, carry):
        u_copy(i).wait_send()
        s_copy(i).wait_send()
        return carry

    lax.fori_loop(1, nz, far_wait, 0)
    for i in range(1, nx):
        tx_copy(i).wait_send()
        q_copy(i).wait_send()
        l_copy(i).wait_send()
        for p in range(PARTS):
            o_copy(i, p).wait_send()
            for layer in range(2):
                a_copy(layer, i, p).wait_send()


    for i in range(nx):
        for layer in range(2):
            for p in range(PARTS):
                forward(layer, i, p).wait_send()
    for stream in range(2):
        for way in range(2):
            for s in range(1, last_step(stream, way) + 1):
                if s > direct:
                    kv_copy(stream, way, s).wait_send()
                w_copy(stream, way, s).wait_send()

    for layer, out in ((0, lo), (1, so)):
        for p in range(PARTS):
            for i in range(1, ny):
                src = (y + i) % ny
                landed(cland.at[layer, src, tokens(p)], cs_r.at[layer, p, src])

            @pl.when(jnp.logical_not(on_diag))
            def _(layer=layer, p=p):
                landed(cland.at[layer, y, tokens(p)], cs_r.at[layer, p, y])

        out[...] = sum(cland[layer, i].astype(F32) for i in range(ny)).astype(BF)

    for layer in range(2):
        for p in range(PARTS):
            for i in range(1, nx):
                c_copy(layer, i, p).wait_send()

            @pl.when(jnp.logical_not(on_diag))
            def _(layer=layer, p=p):
                c_copy(layer, 0, p).wait_send()


def local(nx, nz, *args):
    rows = args[-1].shape[0]
    ny = nx
    half = nz // 2
    sub = TOK // ny
    depth = H * D
    part = depth // nz
    args = list(args)
    args[8] = args[8].reshape(1, depth)
    args[9] = args[9].reshape(1, depth)
    vmem = pl.BlockSpec(memory_space=pltpu.VMEM)
    specs = [pl.BlockSpec(memory_space=pltpu.HBM)] * 12
    specs[4] = pl.BlockSpec(memory_space=pltpu.SMEM)
    dma = pltpu.SemaphoreType.DMA
    scratch = [
        pltpu.VMEM((TOK, depth), BF),
        pltpu.VMEM((TOK, depth), BF),
        pltpu.VMEM((TOK, depth), BF),
        pltpu.VMEM((H, D, D), F32),
        pltpu.VMEM((1, depth), F32),
        pltpu.VMEM((1, depth), F32),
        pltpu.VMEM((rows, args[10].shape[1]), BF),
        pltpu.VMEM((rows, args[10].shape[1]), BF),
        dma((2 * ny + H + 8,)),
        pltpu.VMEM((ny, 2, sub, D), BF),
        pltpu.VMEM((2, nx, nz, sub, D), BF),
        pltpu.VMEM((nx, H, TOK, D), BF),
        pltpu.VMEM((nz, part, D), F32),
        pltpu.VMEM((H, TOK, D), F32),
        pltpu.VMEM((nx, depth, D), F32),
        pltpu.VMEM((nx, depth, D), F32),
        pltpu.VMEM((nx, depth, D), F32),
        pltpu.VMEM((ny, 2, 2, rows, NOUT), F32),
        pltpu.VMEM((2, nx, 2, rows, NOUT), F32),
        pltpu.VMEM((2, 2, nz, nx * rows, NOUT), BF),
        pltpu.VMEM((nz, part, D), BF),
        pltpu.VMEM((nz, part, D), BF),
        pltpu.VMEM((nx, part, D), F32),
        pltpu.VMEM((nz, part, D), BF),
        pltpu.VMEM((nz, part, D), BF),
        pltpu.VMEM((nx, PARTS, H, TOK // PARTS, D), BF),
        pltpu.VMEM((nx, PARTS, H, TOK // PARTS, D), BF),
        pltpu.VMEM((nx, 8, D), F32),
        pltpu.VMEM((ny, 8, D), F32),
        pltpu.VMEM((2, 2, nx, TOK, depth), BF),
        pltpu.VMEM((2, nx, TOK, NOUT), BF),
        pltpu.VMEM((2, nx, TOK, NOUT), BF),
        pltpu.VMEM((depth, depth), BF),
        pltpu.VMEM((TOK, nz * sub), F32),
    ]
    sems = [
        (5, nx), (5, nx), (2, nx), (2, nx), (nx,), (nx,),
        (nz,), (nz,), (nx,), (nx,), (nz,), (nz,),
        (2, 2, half), (2, 2, half), (2, 2, half), (2, 2, half),
        (PARTS, nx), (PARTS, nx), (nx,), (nx,), (2, PARTS, nx), (2, PARTS, nx),
        (2, PARTS, nx), (2, PARTS, nx), (2, PARTS, nx), (2, PARTS, nx),
    ]
    out = jax.ShapeDtypeStruct((TOK, NOUT), BF)
    return pl.pallas_call(
        functools.partial(kernel, nx, nz),
        out_shape=(out, out),
        in_specs=specs,
        out_specs=(vmem, vmem),
        scratch_shapes=scratch + [dma(s) for s in sems],
        compiler_params=pltpu.CompilerParams(
            collective_id=0, has_side_effects=True, vmem_limit_bytes=60 * 1024 * 1024
        ),
        name="plane_attention",
    )(*args)


def solution(mesh):
    nx = mesh.shape["head"] // 2
    nz = mesh.shape["ctx"] // nx
    placed = (
        P("ctx", "head"),
        P("ctx", "head"),
        P("ctx", "head"),
        P("head", None, None),
        P("head"),
        P("ctx", "head"),
        P("ctx", "head"),
        P("ctx", "head"),
        P("head"),
        P("head"),
        P(("head", "ctx"), None),
        P(("head", "ctx"), None),
    )
    return jax.shard_map(
        functools.partial(local, nx, nz),
        mesh=mesh,
        in_specs=placed,
        out_specs=(P("ctx", "head"), P("ctx", "head")),
        check_vma=False,
    )
```
